512 devices in a mesh: dp: 64 (over z, x), tensor: 8 (over y, core).
Axes of the slice: x: 4, y: 4, z: 16, core: 2. Of those that a mesh axis runs over, the one named last changes fastest.
Arguments:
- x_quant: bfloat16 [12288, 8192], P('dp', 'tensor'), may hold values from -6 to 6
- x_scale: float32 [12288, 64], P('dp', 'tensor'), may hold values from 0.1 to 30
- key_quant: bfloat16 [8192, 1024], P('tensor', 'dp'), may hold values from -0.0625 to 0.0625
- key_scale: float32 [64, 1024], P('tensor', 'dp'), may hold values from 0.1 to 20
- value_quant: bfloat16 [8192, 1024], P('tensor', 'dp'), may hold values from -0.0625 to 0.0625
- value_scale: float32 [64, 1024], P('tensor', 'dp'), may hold values from 0.1 to 20
- grad_key: bfloat16 [12288, 1024], P('dp', 'tensor'), may hold values from -1000 to 1000
- grad_value: bfloat16 [12288, 1024], P('dp', 'tensor'), may hold values from -1000 to 1000
Outputs:
- grad_input: bfloat16 [12288, 8192], P('dp', 'tensor')
- grad_key_weight: bfloat16 [8192, 1024], P('tensor', 'dp')
- grad_value_weight: bfloat16 [8192, 1024], P('tensor', 'dp')
- peaks: float32 [2], replicated
- cotangent_peak: float32 [1], replicated
The draws below stay inside these ranges and needn't reach their ends.
All inputs are finite; a program needn't handle non-finite values. Where the reference program divides by a largest or mean magnitude, that divisor is 1e-20 or more.
Results may differ from the reference program's by a relative error of at most 0.0059.
Values may be sent and summed in bfloat16 or wider, within the bound.
No kernel may reach another device: no remote copies, remote signals or barrier semaphores. Data moves between devices by JAX's collectives and lax.ppermute only.
A program may use at most 64 MiB of HBM per device.

```python
import jax
import jax.numpy as jnp
from jax import lax

D = 8192
BLOCK = 128
TOK_DEV = 192
KVW = 1024
TOKENS = 12288
N_DP = 64


def ramp_along(count, summit):
    return summit ** (jnp.arange(count, dtype=jnp.float32) / max(count - 1, 1))


def weight_scales(key, summit):
    base_draw = jnp.exp(jax.random.uniform(key, (D // BLOCK, KVW), jnp.float32, jnp.log(0.5), jnp.log(2.0)))
    return base_draw * ramp_along(D // BLOCK, summit)[:, None]


def shape_grads(key, base_draw, summit):
    row_key, col_key, pair_key = jax.random.split(key, 3)
    row_scale = jnp.exp(jax.random.uniform(row_key, (TOKENS, 1), jnp.float32, 0.0, jnp.log(10.0)))
    col_scale = jnp.exp(jax.random.uniform(col_key, (1, KVW), jnp.float32, 0.0, jnp.log(10.0)))
    col_scale = col_scale * ramp_along(KVW, summit)[None, :]
    groups = TOKENS // TOK_DEV
    pairing = jax.random.permutation(pair_key, groups)
    row_group = jnp.arange(TOKENS) // TOK_DEV
    col_piece = jnp.arange(KVW) // (KVW // groups)
    spike_gain = jnp.where(pairing[row_group][:, None] == col_piece[None, :], 4.0, 1.0)
    return (base_draw * row_scale * col_scale * spike_gain / 30.0).astype(jnp.bfloat16)


def draw_x_scale(key, part):
    key = jax.random.fold_in(key, 11)
    summit = 3.0
    base_draw = jnp.exp(jax.random.uniform(key, (TOKENS, D // BLOCK), jnp.float32, jnp.log(0.3), jnp.log(3.0)))
    return base_draw * ramp_along(D // BLOCK, summit)[None, :]


def draw_key_scale(key, part):
    key = jax.random.fold_in(key, 21)
    summit = 3.0
    return weight_scales(key, summit)


def draw_value_scale(key, part):
    key = jax.random.fold_in(key, 22)
    summit = 3.0
    return weight_scales(key, summit)


def draw_grad_key(key, part):
    key = jax.random.fold_in(key, 31)
    base_draw = jnp.clip(jax.random.normal(key, (TOKENS, KVW), jnp.float32), -6.0, 6.0)
    summit = 3.0
    return shape_grads(jax.random.fold_in(key, 7), base_draw, summit)


def draw_grad_value(key, part):
    key = jax.random.fold_in(key, 32)
    base_draw = jnp.clip(jax.random.normal(key, (TOKENS, KVW), jnp.float32), -6.0, 6.0)
    summit = 3.0
    return shape_grads(jax.random.fold_in(key, 7), base_draw, summit)


def steps_of(stream_key, extent, cuts, smallest, top_value):
    def one(position, parts):
        heights = jax.random.uniform(jax.random.fold_in(jax.random.fold_in(stream_key, 6), position), (parts,), jnp.float32, smallest / len(cuts), top_value / len(cuts))
        return jnp.repeat(jnp.exp(heights), extent[position] // parts).reshape((-1,) + (1,) * (len(extent) - position - 1))

    level = one(*cuts[0])
    for cut in cuts[1:]:
        level = level * one(*cut)
    return level


def normal_values(key, extent, spread, reach, cuts=(), kind=jnp.bfloat16):
    drawn = jax.random.normal(key, extent, jnp.float32) * spread
    if len(cuts) > 0:
        drawn = steps_of(key, extent, cuts, -0.22, 0.18) * drawn
    return jnp.clip(drawn, min=-reach, max=reach).astype(kind)


def setup_inputs(seed: int = 0) -> dict:
    arg_keys = jax.random.split(jax.random.key(seed), 9)
    x_quant = normal_values(arg_keys[0], (TOKENS, D), 1.0, 6.0, ((0, 64), (1, 8)))
    x_scale = draw_x_scale(jax.random.fold_in(arg_keys[8], 71), 0)
    key_quant = normal_values(arg_keys[2], (D, KVW), D ** -0.5, 0.0625, ((0, 8), (1, 64)))
    key_scale = draw_key_scale(jax.random.fold_in(arg_keys[8], 71), 0)
    value_quant = normal_values(arg_keys[4], (D, KVW), D ** -0.5, 0.0625, ((0, 8), (1, 64)))
    value_scale = draw_value_scale(jax.random.fold_in(arg_keys[8], 71), 0)
    grad_key = draw_grad_key(jax.random.fold_in(arg_keys[8], 71), 0)
    grad_value = draw_grad_value(jax.random.fold_in(arg_keys[8], 71), 0)
    return {"x_quant": x_quant, "x_scale": x_scale, "key_quant": key_quant, "key_scale": key_scale, "value_quant": value_quant, "value_scale": value_scale, "grad_key": grad_key, "grad_value": grad_value}


def dequant_rows(quantized, scales):
    row_count, col_count = quantized.shape
    scaled = quantized.astype(jnp.float32).reshape(row_count // BLOCK, BLOCK, col_count) * scales[:, None, :]
    return scaled.reshape(row_count, col_count).astype(jnp.bfloat16)


def dequant_cols(quantized, scales):
    row_count, col_count = quantized.shape
    scaled = quantized.astype(jnp.float32).reshape(row_count, col_count // BLOCK, BLOCK) * scales[:, :, None]
    return scaled.reshape(row_count, col_count).astype(jnp.bfloat16)


def contract_rows(former, latter):
    return lax.dot_general(former, latter, (((0,), (0,)), ((), ())), preferred_element_type=jnp.float32)


def contract_cols(former, latter):
    return lax.dot_general(former, latter, (((1,), (1,)), ((), ())), preferred_element_type=jnp.float32)


def block_restore(partial_value, pieces):
    row_count, col_count = partial_value.shape
    blocks = partial_value.reshape(row_count // BLOCK, BLOCK, pieces, col_count // pieces)
    block_peak = jnp.max(jnp.abs(blocks), axis=(1, 3)) + 1e-6
    quantized = (blocks / block_peak[:, None, :, None]).astype(jnp.bfloat16)
    restored = quantized.astype(jnp.float32) * block_peak[:, None, :, None]
    return restored.reshape(row_count, col_count)


def reference(x_quant, x_scale, key_quant, key_scale, value_quant, value_scale, grad_key, grad_value):
    key_weight = dequant_rows(key_quant, key_scale)
    value_weight = dequant_rows(value_quant, value_scale)
    input_sum = contract_cols(grad_key, key_weight) + contract_cols(grad_value, value_weight)
    input_peak = jnp.max(jnp.abs(input_sum)) + 1e-6
    grad_input = (input_sum / input_peak).astype(jnp.bfloat16)
    pieces = N_DP

    def group_step(running, group_idx):
        offset = (group_idx * TOK_DEV).astype(jnp.int32)
        inputs = dequant_cols(lax.dynamic_slice_in_dim(x_quant, offset, TOK_DEV, 0),
                              lax.dynamic_slice_in_dim(x_scale, offset, TOK_DEV, 0))
        key_part = contract_rows(inputs, lax.dynamic_slice_in_dim(grad_key, offset, TOK_DEV, 0))
        value_part = contract_rows(inputs, lax.dynamic_slice_in_dim(grad_value, offset, TOK_DEV, 0))
        return (running[0] + block_restore(key_part, pieces), running[1] + block_restore(value_part, pieces)), None

    zeros_init = jnp.zeros((D, KVW), jnp.float32)
    sums, unused = lax.scan(group_step, (zeros_init, zeros_init), jnp.arange(pieces, dtype=jnp.int32))
    key_sum, value_sum = sums
    key_peak = jnp.max(jnp.abs(key_sum)) + 1e-6
    value_peak = jnp.max(jnp.abs(value_sum)) + 1e-6
    grad_key_weight = (key_sum / key_peak).astype(jnp.bfloat16)
    grad_value_weight = (value_sum / value_peak).astype(jnp.bfloat16)
    peaks = jnp.stack([key_peak, value_peak])
    cotangent_peak = jnp.reshape(input_peak, (1,))
    return grad_input, grad_key_weight, grad_value_weight, peaks, cotangent_peak
```

```python
import jax
import jax.numpy as jnp
from jax import lax
from jax.sharding import Mesh, PartitionSpec as P

BLOCK = 128
DP = ("zh", "zl", "x")
TENSOR = ("y", "c")
F32, BF16 = jnp.float32, jnp.bfloat16


def spread(block, axes):
    count = lax.axis_size(axes)
    copies = jnp.broadcast_to(block[None], (count, *block.shape))
    return lax.all_to_all(copies, axes, 0, 0, tiled=True)


def per_device(
    x_quant, x_scale, key_quant, key_scale, value_quant, value_scale, grad_key, grad_value
):
    tokens, features = x_quant.shape
    cols = key_quant.shape[1]
    nx = lax.axis_size("x")
    nzh, nzl = lax.axis_size("zh"), lax.axis_size("zl")

    grads = jnp.stack([grad_key.T, grad_value.T])
    grads = grads.reshape(2, 2, nx, cols, tokens).transpose(2, 1, 0, 3, 4)
    grads = grads.reshape(nx, 1, 4 * cols, tokens)
    grads = jnp.broadcast_to(grads, (nx, lax.axis_size(TENSOR), 4 * cols, tokens))
    grads = lax.all_to_all(
        grads.reshape(-1, 4 * cols, tokens), ("x", *TENSOR), 0, 0, tiled=True
    )
    grads = grads.reshape(nx, nzh, 2, 2, 2 * cols, tokens)
    grads = grads.transpose(0, 2, 3, 1, 4, 5).reshape(nx, nzl * nzh * 2 * cols, tokens)

    inputs = x_quant.astype(F32).reshape(tokens, features // BLOCK, BLOCK)
    inputs = (inputs * x_scale[:, :, None]).astype(BF16).reshape(tokens, features)
    inputs = spread(inputs, "x")

    weight = jnp.stack([key_quant.T, value_quant.T]).astype(F32)
    scale = jnp.stack([key_scale.T, value_scale.T])
    weight = weight.reshape(2, cols, features // BLOCK, BLOCK) * scale[..., None]
    weight = weight.astype(BF16).reshape(2 * cols, features)
    weight = spread(weight, "zh").reshape(nzh * 2 * cols, features)
    weight = spread(weight, "zl").reshape(nzl * nzh * 2 * cols, features)

    part = jnp.einsum("xct,xtd->cd", grads, inputs, preferred_element_type=F32)
    part = part.astype(BF16).reshape(nzl, nzh * 2 * cols, features)
    part = lax.all_to_all(part, "zl", 0, 0, tiled=True)
    part = jnp.sum(part.astype(F32), axis=0).astype(BF16)
    part = part.reshape(nzh, 2 * cols, features)
    part = lax.all_to_all(part, "zh", 0, 0, tiled=True)
    weight_sum = jnp.sum(part.astype(F32), axis=0).reshape(2, cols, features)
    weight_peak = jnp.max(jnp.abs(weight_sum), axis=(1, 2))

    part = jnp.einsum("xct,cd->xtd", grads, weight, preferred_element_type=F32)
    part = lax.all_to_all(part.astype(BF16), "x", 0, 0, tiled=True)
    input_sum = jnp.sum(part.astype(F32), axis=0)
    input_peak = jnp.max(jnp.abs(input_sum))

    peaks = jnp.concatenate([weight_peak, input_peak[None]])
    peaks = jnp.pad(peaks, (0, 125))
    peaks = jnp.max(spread(peaks, DP), axis=0)
    peaks = jnp.max(spread(peaks, TENSOR), axis=0) + 1e-06
    grad_weight = (weight_sum / peaks[:2, None, None]).astype(BF16)
    grad_input = (input_sum / peaks[2]).astype(BF16)
    return (grad_input, grad_weight[0].T, grad_weight[1].T, peaks[:2], peaks[2:3])


def solution(mesh):
    whole = Mesh(mesh.devices.reshape(4, 4, 4, 4, 2), (*DP, *TENSOR))
    in_specs = (
        P(DP, TENSOR),
        P(DP, TENSOR),
        P(TENSOR, DP),
        P(TENSOR, DP),
        P(TENSOR, DP),
        P(TENSOR, DP),
        P(DP, TENSOR),
        P(DP, TENSOR),
    )
    out_specs = (P(DP, TENSOR), P(TENSOR, DP), P(TENSOR, DP), P(), P())
    return jax.shard_map(
        per_device, mesh=whole, in_specs=in_specs, out_specs=out_specs, check_vma=False
    )
```

```python
import jax
import jax.numpy as jnp
from jax import lax
from jax.experimental import pallas as pl
from jax.experimental.pallas import tpu as pltpu
from jax.sharding import Mesh, PartitionSpec as P

BLOCK = 128
DP = ("zh", "zl", "x")
TENSOR = ("y", "c")
RING = ("zh", "zl")
F32, BF16 = jnp.float32, jnp.bfloat16
VMEM = pl.BlockSpec(memory_space=pltpu.VMEM)
SMEM = pl.BlockSpec(memory_space=pltpu.SMEM)


def kernel_call(body, out_shape, in_specs, out_specs=None, scratch=(), flops=0):
    if out_specs is None:
        out_specs = jax.tree.map(lambda _: VMEM, out_shape)
    return pl.pallas_call(
        body,
        out_shape=out_shape,
        in_specs=in_specs,
        out_specs=out_specs,
        scratch_shapes=list(scratch),
        cost_estimate=pl.CostEstimate(flops=flops, bytes_accessed=0, transcendentals=0),
        compiler_params=pltpu.CompilerParams(vmem_limit_bytes=40 * 2**20),
    )


def shape(dims, dtype):
    return jax.ShapeDtypeStruct(dims, dtype)


def shift(value, axes, by):
    count = lax.axis_size(axes)
    return lax.ppermute(value, axes, [(i, (i + by) % count) for i in range(count)])


def spread(block, axes):
    count = lax.axis_size(axes)
    copies = jnp.broadcast_to(block[None], (count, *block.shape))
    return lax.all_to_all(copies, axes, 0, 0, tiled=True)


def grads_body(key_ref, value_ref, out_ref):
    key, value = key_ref[...].T, value_ref[...].T
    for x in range(4):
        rows = []
        for zz in range(2):
            start = zz * 64 + x * 16
            rows += [key[start : start + 16], value[start : start + 16]]
        block = jnp.concatenate(rows, axis=0)
        for copy in range(4):
            out_ref[x, copy] = block


def scale_body(x_ref, x_scale_ref, key_ref, key_scale_ref, value_ref, value_scale_ref, out_ref, weight_ref):
    for b in range(8):
        at = slice(b * BLOCK, (b + 1) * BLOCK)
        out_ref[:, at] = (x_ref[:, at].astype(F32) * x_scale_ref[:, b : b + 1]).astype(BF16)
        for part, ref, scale in ((0, key_ref, key_scale_ref), (1, value_ref, value_scale_ref)):
            weight_ref[part * 16 : (part + 1) * 16, at] = (
                ref[:, at].astype(F32) * scale[:, b : b + 1]
            ).astype(BF16)


def weight_body(place, own_ref, twin_ref, x0, x1, x2, x3, keep_ref, out1, out2a, out2b, out3, total):
    x, zl, core = place[0], place[1], place[2]
    for i, part in enumerate((own_ref, twin_ref)):
        value = None
        for ref, back in ((x0, 0), (x1, 1), (x2, 2), (x3, 3)):
            lhs = part[lax.rem(x + 4 - back, 4)]
            term = jnp.dot(lhs, ref[...], preferred_element_type=F32)
            value = term if value is None else value + term
        total[i] = value.reshape(4, 2, 32, 1024)
    for k, out in enumerate((keep_ref, out1, None, out3)):
        group = lax.rem(zl + k, 4)
        half, zz = lax.rem(group // 2 + core, 2), lax.rem(group, 2)
        for y in range(4):
            block = total[half, y, zz]
            if k == 2:
                target = (out2a, out2b)[y // 2]
                target[(y % 2) * 32 : (y % 2 + 1) * 32] = block.astype(BF16)
            else:
                out[y * 32 : (y + 1) * 32] = block.astype(out.dtype)


def input_body(place, own_ref, twin_ref, w0, w1, w2, w3, keep_ref, out1, out2, out3, weight):
    x, zl, core = place[0], place[1], place[2]
    for back, ref in enumerate((w0, w1, w2, w3)):
        group = lax.rem(zl + 4 - back, 4)
        half, zz = lax.rem(group // 2 + core, 2), lax.rem(group, 2)
        for y in range(4):
            weight[half, y, zz] = ref[y * 32 : (y + 1) * 32]
    for k, out in enumerate((keep_ref, out1, out2, out3)):
        member = lax.rem(x + k, 4)
        value = jnp.dot(
            own_ref[member].T, weight[0].reshape(256, 1024), preferred_element_type=F32
        ) + jnp.dot(
            twin_ref[member].T, weight[1].reshape(256, 1024), preferred_element_type=F32
        )
        out[...] = value.astype(out.dtype)


def near_body(keep_ref, r1, r2a, r2b, r3, out_ref):
    for i, r2 in enumerate((r2a, r2b)):
        at = slice(i * 64, (i + 1) * 64)
        total = keep_ref[at] + r1[at].astype(F32) + r2[...].astype(F32) + r3[at].astype(F32)
        out_ref[i * 2 : (i + 1) * 2] = total.astype(BF16).reshape(2, 32, 1024)


def peak_body(far_ref, keep_ref, r1, r2, r3, weight_ref, input_ref, peak_ref):
    weight = far_ref[0].astype(F32)
    for i in range(1, 4):
        weight = weight + far_ref[i].astype(F32)
    weight_ref[...] = weight
    total = keep_ref[...] + r1[...].astype(F32) + r2[...].astype(F32) + r3[...].astype(F32)
    input_ref[...] = total
    size = jnp.abs(weight)
    lane = lax.broadcasted_iota(jnp.int32, peak_ref.shape, 1)
    peak_ref[...] = jnp.where(
        lane == 0,
        jnp.max(size[:16]),
        jnp.where(lane == 1, jnp.max(size[16:]), jnp.max(jnp.abs(total))),
    )


def final_body(peaks_ref, weight_ref, input_ref, out_ref, key_ref, value_ref, pair_ref, one_ref):
    peaks = jnp.max(peaks_ref[...], axis=0, keepdims=True) + 1e-06
    key_peak, value_peak, input_peak = peaks[0, 0], peaks[0, 1], peaks[0, 2]
    key_ref[...] = (weight_ref[:16] / key_peak).astype(BF16)
    value_ref[...] = (weight_ref[16:] / value_peak).astype(BF16)
    out_ref[...] = (input_ref[...] / input_peak).astype(BF16)
    pair_ref[0] = key_peak
    pair_ref[1] = value_peak
    one_ref[0] = input_peak


def per_device(
    x_quant, x_scale, key_quant, key_scale, value_quant, value_scale, grad_key, grad_value
):
    place = jnp.stack([lax.axis_index(axis) for axis in ("x", "zl", "c")]).astype(jnp.int32)

    own = kernel_call(grads_body, shape((4, 4, 64, 192), BF16), [VMEM] * 2)(grad_key, grad_value)
    own = lax.all_to_all(own.reshape(16, 64, 192), ("x", "y"), 0, 0, tiled=True)
    own = own.reshape(4, 256, 192)
    twin = lax.ppermute(own, "c", [(0, 1), (1, 0)])

    inputs, weight = kernel_call(
        scale_body, (shape((192, 1024), BF16), shape((32, 1024), BF16)), [VMEM] * 6
    )(x_quant, x_scale, key_quant.T, key_scale.T, value_quant.T, value_scale.T)
    others = [shift(inputs, "x", by) for by in (1, 2, 3)]

    own, weight = lax.optimization_barrier((own, weight))
    weight = spread(weight, "zh").reshape(128, 1024)

    keep, *parts = kernel_call(
        weight_body,
        (shape((128, 1024), F32), shape((128, 1024), BF16))
        + (shape((64, 1024), BF16),) * 2
        + (shape((128, 1024), BF16),),
        [SMEM] + [VMEM] * 6,
        scratch=[pltpu.VMEM((2, 4, 2, 32, 1024), F32)],
        flops=10**11,
    )(place, own, twin, inputs, *others)
    parts = [shift(part, RING, by) for part, by in zip(parts, (1, 2, -2, -1))]
    weights = [weight] + [shift(weight, RING, by) for by in (1, 2, -1)]
    part = kernel_call(near_body, shape((4, 32, 1024), BF16), [VMEM] * 5)(keep, *parts)
    far = lax.all_to_all(part, "zh", 0, 0, tiled=True)

    keep, *parts = kernel_call(
        input_body,
        (shape((192, 1024), F32),) + (shape((192, 1024), BF16),) * 3,
        [SMEM] + [VMEM] * 6,
        scratch=[pltpu.VMEM((2, 4, 2, 32, 1024), BF16)],
        flops=10**11,
    )(place, own, twin, *weights)
    parts = [shift(part, "x", by) for part, by in zip(parts, (1, 2, 3))]

    weight_sum, input_sum, peaks = kernel_call(
        peak_body,
        (shape((32, 1024), F32), shape((192, 1024), F32), shape((64, 128), F32)),
        [VMEM] * 5,
    )(far, keep, *parts)
    peaks = lax.all_to_all(peaks, DP, 0, 0, tiled=True)
    peaks = spread(jnp.max(peaks, axis=0), TENSOR)
    grad_input, grad_key_weight, grad_value_weight, pair, one = kernel_call(
        final_body,
        (
            shape((192, 1024), BF16),
            shape((16, 1024), BF16),
            shape((16, 1024), BF16),
            shape((2,), F32),
            shape((1,), F32),
        ),
        [VMEM] * 3,
        (VMEM, VMEM, VMEM, SMEM, SMEM),
    )(peaks.reshape(8, 128), weight_sum, input_sum)
    return (grad_input, grad_key_weight.T, grad_value_weight.T, pair, one)


def solution(mesh):
    whole = Mesh(mesh.devices.reshape(4, 4, 4, 4, 2), (*DP, *TENSOR))
    in_specs = (
        P(DP, TENSOR),
        P(DP, TENSOR),
        P(TENSOR, DP),
        P(TENSOR, DP),
        P(TENSOR, DP),
        P(TENSOR, DP),
        P(DP, TENSOR),
        P(DP, TENSOR),
    )
    out_specs = (P(DP, TENSOR), P(TENSOR, DP), P(TENSOR, DP), P(), P())
    return jax.shard_map(
        per_device, mesh=whole, in_specs=in_specs, out_specs=out_specs, check_vma=False
    )
```

```python
import jax
import jax.numpy as jnp
from jax import lax
from jax.experimental import pallas as pl
from jax.experimental.pallas import tpu as pltpu
from jax.sharding import Mesh, PartitionSpec as P

BLOCK = 128
DP = ("zh", "zm", "zp", "x")
TENSOR = ("y", "c")
RING = ("zh", "zm", "zp")
F32, BF16 = jnp.float32, jnp.bfloat16
VMEM = pl.BlockSpec(memory_space=pltpu.VMEM)
SMEM = pl.BlockSpec(memory_space=pltpu.SMEM)


def kernel_call(body, out_shape, in_specs, out_specs=None, scratch=(), flops=0):
    if out_specs is None:
        out_specs = jax.tree.map(lambda _: VMEM, out_shape)
    return pl.pallas_call(
        body,
        out_shape=out_shape,
        in_specs=in_specs,
        out_specs=out_specs,
        scratch_shapes=list(scratch),
        cost_estimate=pl.CostEstimate(flops=flops, bytes_accessed=0, transcendentals=0),
        compiler_params=pltpu.CompilerParams(vmem_limit_bytes=16 * 2**20),
    )


def shape(dims, dtype):
    return jax.ShapeDtypeStruct(dims, dtype)


def shift(value, axes, by):
    count = lax.axis_size(axes)
    return lax.ppermute(value, axes, [(i, (i + by) % count) for i in range(count)])


def spread(block, axes):
    count = lax.axis_size(axes)
    copies = jnp.broadcast_to(block[None], (count, *block.shape))
    return lax.all_to_all(copies, axes, 0, 0, tiled=True)


def grads_body(key_ref, value_ref, out_ref):
    key, value = key_ref[...].T, value_ref[...].T
    for x in range(4):
        rows = []
        for zz in range(2):
            start = zz * 64 + x * 16
            rows += [key[start : start + 16], value[start : start + 16]]
        block = jnp.concatenate(rows, axis=0)
        for copy in range(4):
            out_ref[x, copy] = block


def scale_body(x_ref, x_scale_ref, key_ref, key_scale_ref, value_ref, value_scale_ref, out_ref, weight_ref):
    for b in range(8):
        at = slice(b * BLOCK, (b + 1) * BLOCK)
        out_ref[:, at] = (x_ref[:, at].astype(F32) * x_scale_ref[:, b : b + 1]).astype(BF16)
        for part, ref, scale in ((0, key_ref, key_scale_ref), (1, value_ref, value_scale_ref)):
            weight_ref[part * 16 : (part + 1) * 16, at] = (
                ref[:, at].astype(F32) * scale[:, b : b + 1]
            ).astype(BF16)


def weight_body(place, own, twin, x0, x1, x2, x3, keep_ref, key_ref, value_ref, total):
    x, zp, core = place[0], place[2], place[3]
    inputs = jnp.concatenate([ref[...] for ref in (x0, x1, x2, x3)], axis=0)
    for i, part in enumerate((own, twin)):
        lhs = jnp.concatenate([part[lax.rem(x + 4 - back, 4)] for back in range(4)], axis=1)
        value = jnp.dot(lhs, inputs, preferred_element_type=F32)
        total[i] = value.reshape(4, 2, 32, 1024)
        zm = lax.rem(core + i, 2)
        for zh in range(4):
            keep_ref[zh, zm] = total[i, zh, zp]
            key_ref[zh, zm] = total[i, zh, 1 - zp, :16].astype(BF16)
            value_ref[zh, zm] = total[i, zh, 1 - zp, 16:].astype(BF16)


def input_body(place, own, twin, w0, w1, w2, w3, keep_ref, out1, out2a, out2b, out3, weight):
    x, zl, core = place[0], place[1] * 2 + place[2], place[3]
    for back, ref in enumerate((w0, w1, w2, w3)):
        group = lax.rem(zl + 4 - back, 4)
        half, zp = lax.rem(group // 2 + core, 2), lax.rem(group, 2)
        for zh in range(4):
            weight[half, zh, zp] = ref[zh]
    for k, out in enumerate((keep_ref, out1, None, out3)):
        member = lax.rem(x + k, 4)
        lhs = jnp.concatenate([own[member].T, twin[member].T], axis=1)
        value = jnp.dot(lhs, weight[...].reshape(512, 1024), preferred_element_type=F32)
        if k == 2:
            out2a[...] = value[:96].astype(BF16)
            out2b[...] = value[96:].astype(BF16)
        else:
            out[...] = value.astype(out.dtype)


def near_body(keep_ref, key_ref, value_ref, out_ref):
    for zh in range(4):
        for zm in range(2):
            keep = keep_ref[zh, zm]
            out_ref[zh * 2 + zm, :16] = (keep[:16] + key_ref[zh, zm].astype(F32)).astype(BF16)
            out_ref[zh * 2 + zm, 16:] = (keep[16:] + value_ref[zh, zm].astype(F32)).astype(BF16)


def peak_body(far_ref, keep_ref, r1, r2a, r2b, r3, weight_ref, input_ref, peak_ref):
    weight = far_ref[0].astype(F32)
    for i in range(1, 8):
        weight = weight + far_ref[i].astype(F32)
    weight_ref[...] = weight
    input_peak = None
    for at, r2 in ((slice(0, 96), r2a), (slice(96, 192), r2b)):
        total = keep_ref[at] + r1[at].astype(F32) + r2[...].astype(F32) + r3[at].astype(F32)
        input_ref[at] = total
        peak = jnp.max(jnp.abs(total))
        input_peak = peak if input_peak is None else jnp.maximum(input_peak, peak)
    size = jnp.abs(weight)
    lane = lax.broadcasted_iota(jnp.int32, peak_ref.shape, 1)
    peak_ref[...] = jnp.where(
        lane == 0,
        jnp.max(size[:16]),
        jnp.where(lane == 1, jnp.max(size[16:]), input_peak),
    )


def final_body(peaks_ref, weight_ref, input_ref, out_ref, key_ref, value_ref, pair_ref, one_ref):
    peaks = jnp.max(peaks_ref[...], axis=0, keepdims=True) + 1e-06
    key_peak, value_peak, input_peak = peaks[0, 0], peaks[0, 1], peaks[0, 2]
    key_ref[...] = (weight_ref[:16] / key_peak).astype(BF16)
    value_ref[...] = (weight_ref[16:] / value_peak).astype(BF16)
    out_ref[...] = (input_ref[...] / input_peak).astype(BF16)
    pair_ref[0] = key_peak
    pair_ref[1] = value_peak
    one_ref[0] = input_peak


def per_device(
    x_quant, x_scale, key_quant, key_scale, value_quant, value_scale, grad_key, grad_value
):
    place = jnp.stack([lax.axis_index(axis) for axis in ("x", "zm", "zp", "c")]).astype(jnp.int32)

    own = kernel_call(
        grads_body,
        shape((4, 4, 64, 192), BF16),
        [VMEM] * 2,
    )(grad_key, grad_value)
    own = lax.all_to_all(own.reshape(16, 64, 192), ("x", "y"), 0, 0, tiled=True)
    own = own.reshape(4, 256, 192)
    twin = lax.ppermute(own, "c", [(0, 1), (1, 0)])

    inputs, weight = kernel_call(
        scale_body, (shape((192, 1024), BF16), shape((32, 1024), BF16)), [VMEM] * 6
    )(x_quant, x_scale, key_quant.T, key_scale.T, value_quant.T, value_scale.T)
    others = [shift(inputs, "x", by) for by in (1, 2, 3)]

    own, weight = lax.optimization_barrier((own, weight))
    weight = spread(weight, "zh")

    keep, key, value = kernel_call(
        weight_body,
        (shape((4, 2, 32, 1024), F32),) + (shape((4, 2, 16, 1024), BF16),) * 2,
        [SMEM] + [VMEM] * 6,
        scratch=[pltpu.VMEM((2, 4, 2, 32, 1024), F32)],
        flops=10**11,
    )(place, own, twin, inputs, *others)
    key, value = shift(key, RING, -1), shift(value, RING, 1)
    weights = [weight] + [shift(weight, RING, by) for by in (1, -2, -1)]
    part = kernel_call(near_body, shape((8, 32, 1024), BF16), [VMEM] * 3)(keep, key, value)
    far = lax.all_to_all(part, ("zh", "zm"), 0, 0, tiled=True)

    block, half = shape((192, 1024), BF16), shape((96, 1024), BF16)
    keep, *parts = kernel_call(
        input_body,
        (shape((192, 1024), F32), block, half, half, block),
        [SMEM] + [VMEM] * 6,
        scratch=[pltpu.VMEM((2, 4, 2, 32, 1024), BF16)],
        flops=10**11,
    )(place, own, twin, *weights)
    parts = [shift(part, "x", by) for part, by in zip(parts, (1, 2, -2, -1))]

    weight_sum, input_sum, peaks = kernel_call(
        peak_body,
        (shape((32, 1024), F32), shape((192, 1024), F32), shape((64, 128), F32)),
        [VMEM] * 6,
    )(far, keep, *parts)
    peaks = lax.all_to_all(peaks, DP, 0, 0, tiled=True)
    peaks = spread(jnp.max(peaks, axis=0), TENSOR)
    grad_input, grad_key_weight, grad_value_weight, pair, one = kernel_call(
        final_body,
        (
            shape((192, 1024), BF16),
            shape((16, 1024), BF16),
            shape((16, 1024), BF16),
            shape((2,), F32),
            shape((1,), F32),
        ),
        [VMEM] * 3,
        (VMEM, VMEM, VMEM, SMEM, SMEM),
    )(peaks.reshape(8, 128), weight_sum, input_sum)
    return (grad_input, grad_key_weight.T, grad_value_weight.T, pair, one)


def solution(mesh):
    whole = Mesh(mesh.devices.reshape(4, 2, 2, 4, 4, 2), (*DP, *TENSOR))
    in_specs = (
        P(DP, TENSOR),
        P(DP, TENSOR),
        P(TENSOR, DP),
        P(TENSOR, DP),
        P(TENSOR, DP),
        P(TENSOR, DP),
        P(DP, TENSOR),
        P(DP, TENSOR),
    )
    out_specs = (P(DP, TENSOR), P(TENSOR, DP), P(TENSOR, DP), P(), P())
    return jax.shard_map(
        per_device, mesh=whole, in_specs=in_specs, out_specs=out_specs, check_vma=False
    )
```

```python
import jax
import jax.numpy as jnp
from jax import lax
from jax.experimental import pallas as pl
from jax.experimental.pallas import tpu as pltpu
from jax.sharding import Mesh, PartitionSpec as P

BLOCK = 128
DP = ("zh", "zm", "zp", "x")
TENSOR = ("y", "c")
RING = ("zh", "zm", "zp")
F32, BF16 = jnp.float32, jnp.bfloat16
VMEM = pl.BlockSpec(memory_space=pltpu.VMEM)
SMEM = pl.BlockSpec(memory_space=pltpu.SMEM)
HBM = pl.BlockSpec(memory_space=pltpu.HBM)


def kernel_call(body, out_shape, in_specs, out_specs=None, scratch=(), flops=0):
    if out_specs is None:
        out_specs = jax.tree.map(lambda _: VMEM, out_shape)
    return pl.pallas_call(
        body,
        out_shape=out_shape,
        in_specs=in_specs,
        out_specs=out_specs,
        scratch_shapes=list(scratch),
        cost_estimate=pl.CostEstimate(flops=flops, bytes_accessed=0, transcendentals=0),
        compiler_params=pltpu.CompilerParams(vmem_limit_bytes=16 * 2**20),
    )


def shape(dims, dtype):
    return jax.ShapeDtypeStruct(dims, dtype)


def shift(value, axes, by):
    count = lax.axis_size(axes)
    return lax.ppermute(value, axes, [(i, (i + by) % count) for i in range(count)])


def shift_by_core(value, by):
    count = lax.axis_size(RING)
    pairs = [
        (z * 2 + core, (z + (by, -by)[core]) % count * 2 + core)
        for z in range(count)
        for core in range(2)
    ]
    return lax.ppermute(value, (*RING, "c"), pairs)


def spread(block, axes):
    count = lax.axis_size(axes)
    copies = jnp.broadcast_to(block[None], (count, *block.shape))
    return lax.all_to_all(copies, axes, 0, 0, tiled=True)


def grads_body(key_ref, value_ref, out_ref, key, value, sems):
    copies = [
        pltpu.make_async_copy(source, target, sems.at[i])
        for i, (source, target) in enumerate(((key_ref, key), (value_ref, value)))
    ]
    for copy in copies:
        copy.start()
    for copy in copies:
        copy.wait()
    key, value = key[...].T, value[...].T
    for x in range(4):
        rows = []
        for zz in range(2):
            start = zz * 64 + x * 16
            rows += [key[start : start + 16], value[start : start + 16]]
        block = jnp.concatenate(rows, axis=0)
        for copy in range(4):
            out_ref[x, copy] = block


def scale_body(x_ref, x_scale_ref, key_ref, key_scale_ref, value_ref, value_scale_ref, out_ref, weight_ref):
    for b in range(8):
        at = slice(b * BLOCK, (b + 1) * BLOCK)
        out_ref[:, at] = (x_ref[:, at].astype(F32) * x_scale_ref[:, b : b + 1]).astype(BF16)
        for part, ref, scale in ((0, key_ref, key_scale_ref), (1, value_ref, value_scale_ref)):
            scaled = (ref[:, at].astype(F32) * scale[:, b : b + 1]).astype(BF16)
            for copy in range(4):
                weight_ref[copy, part * 16 : (part + 1) * 16, at] = scaled


def weight_body(place, own, twin, x0, x1, x2, x3, keep_ref, key_ref, value_ref, total):
    x, zp, core = place[0], place[2], place[3]
    inputs = jnp.concatenate([ref[...] for ref in (x0, x1, x2, x3)], axis=0)
    for i, part in enumerate((own, twin)):
        lhs = jnp.concatenate([part[lax.rem(x + 4 - back, 4)] for back in range(4)], axis=1)
        value = jnp.dot(lhs, inputs, preferred_element_type=F32)
        total[i] = value.reshape(4, 2, 32, 1024)
        zm = lax.rem(core + i, 2)
        for zh in range(4):
            keep_ref[zh, zm] = total[i, zh, zp]
            key_ref[zh, zm] = total[i, zh, 1 - zp, :16].astype(BF16)
            value_ref[zh, zm] = total[i, zh, 1 - zp, 16:].astype(BF16)


def input_body(place, own, twin, w0, w1, w2, w3, keep_ref, out1, out2, out3, weight):
    x, zl, core = place[0], place[1] * 2 + place[2], place[3]
    for back, ref in enumerate((w0, w1, w2, w3)):
        group = lax.rem(zl + 4 - back, 4)
        half, zp = lax.rem(group // 2 + core, 2), lax.rem(group, 2)
        for zh in range(4):
            weight[half, zh, zp] = ref[zh]
    for k, out in enumerate((keep_ref, out1, out2, out3)):
        member = lax.rem(x + k, 4)
        lhs = jnp.concatenate([own[member].T, twin[member].T], axis=1)
        out[...] = jnp.dot(
            lhs, weight[...].reshape(512, 1024), preferred_element_type=F32
        ).astype(out.dtype)


def near_body(keep_ref, key_ref, value_ref, out_ref):
    for zh in range(4):
        for zm in range(2):
            keep = keep_ref[zh, zm]
            out_ref[zh * 2 + zm, :16] = (keep[:16] + key_ref[zh, zm].astype(F32)).astype(BF16)
            out_ref[zh * 2 + zm, 16:] = (keep[16:] + value_ref[zh, zm].astype(F32)).astype(BF16)


def peak_body(far_ref, keep_ref, r1, r2, r3, weight_ref, input_ref, peak_ref):
    weight = far_ref[0].astype(F32)
    for i in range(1, 8):
        weight = weight + far_ref[i].astype(F32)
    weight_ref[...] = weight
    total = keep_ref[...] + r1[...].astype(F32) + r2[...].astype(F32) + r3[...].astype(F32)
    input_ref[...] = total
    input_peak = jnp.max(jnp.abs(total))
    size = jnp.abs(weight)
    lane = lax.broadcasted_iota(jnp.int32, peak_ref.shape, 1)
    peak_ref[...] = jnp.where(
        lane == 0,
        jnp.max(size[:16]),
        jnp.where(lane == 1, jnp.max(size[16:]), input_peak),
    )


def final_body(peaks_ref, weight_ref, input_ref, out_ref, key_ref, value_ref, pair_ref, one_ref):
    peaks = jnp.max(peaks_ref[...], axis=0, keepdims=True) + 1e-06
    key_peak, value_peak, input_peak = peaks[0, 0], peaks[0, 1], peaks[0, 2]
    key_ref[...] = (weight_ref[:16] / key_peak).astype(BF16)
    value_ref[...] = (weight_ref[16:] / value_peak).astype(BF16)
    out_ref[...] = (input_ref[...] / input_peak).astype(BF16)
    pair_ref[0] = key_peak
    pair_ref[1] = value_peak
    one_ref[0] = input_peak


def per_device(
    x_quant, x_scale, key_quant, key_scale, value_quant, value_scale, grad_key, grad_value
):
    place = jnp.stack([lax.axis_index(axis) for axis in ("x", "zm", "zp", "c")]).astype(jnp.int32)

    own = kernel_call(
        grads_body,
        shape((4, 4, 64, 192), BF16),
        [HBM] * 2,
        scratch=[pltpu.VMEM((192, 128), BF16)] * 2 + [pltpu.SemaphoreType.DMA((2,))],
    )(grad_key, grad_value)
    own = lax.all_to_all(own.reshape(16, 64, 192), ("x", "y"), 0, 0, tiled=True)
    own = own.reshape(4, 256, 192)
    twin = lax.ppermute(own, "c", [(0, 1), (1, 0)])

    inputs, weight = kernel_call(
        scale_body, (shape((192, 1024), BF16), shape((4, 32, 1024), BF16)), [VMEM] * 6
    )(x_quant, x_scale, key_quant.T, key_scale.T, value_quant.T, value_scale.T)
    others = [shift(inputs, "x", by) for by in (1, 2, 3)]

    own, weight = lax.optimization_barrier((own, weight))
    weight = lax.all_to_all(weight, "zh", 0, 0, tiled=True)

    keep, key, value = kernel_call(
        weight_body,
        (shape((4, 2, 32, 1024), F32),) + (shape((4, 2, 16, 1024), BF16),) * 2,
        [SMEM] + [VMEM] * 6,
        scratch=[pltpu.VMEM((2, 4, 2, 32, 1024), F32)],
        flops=10**11,
    )(place, own, twin, inputs, *others)
    key, value = shift(key, RING, -1), shift(value, RING, 1)
    weights = [weight, shift(weight, RING, 1), shift_by_core(weight, 2), shift(weight, RING, -1)]
    part = kernel_call(near_body, shape((8, 32, 1024), BF16), [VMEM] * 3)(keep, key, value)
    far = lax.all_to_all(part, ("zh", "zm"), 0, 0, tiled=True)

    keep, *parts = kernel_call(
        input_body,
        (shape((192, 1024), F32),) + (shape((192, 1024), BF16),) * 3,
        [SMEM] + [VMEM] * 6,
        scratch=[pltpu.VMEM((2, 4, 2, 32, 1024), BF16)],
        flops=10**11,
    )(place, own, twin, *weights)
    parts = [shift(part, "x", by) for part, by in zip(parts, (1, 2, 3))]

    weight_sum, input_sum, peaks = kernel_call(
        peak_body,
        (shape((32, 1024), F32), shape((192, 1024), F32), shape((32, 128), F32)),
        [VMEM] * 5,
    )(far, keep, *parts)
    peaks = lax.all_to_all(peaks, ("x", *TENSOR), 0, 0, tiled=True)
    peaks = spread(jnp.max(peaks, axis=0), RING)
    grad_input, grad_key_weight, grad_value_weight, pair, one = kernel_call(
        final_body,
        (
            shape((192, 1024), BF16),
            shape((16, 1024), BF16),
            shape((16, 1024), BF16),
            shape((2,), F32),
            shape((1,), F32),
        ),
        [VMEM] * 3,
        (VMEM, VMEM, VMEM, SMEM, SMEM),
    )(peaks.reshape(16, 128), weight_sum, input_sum)
    return (grad_input, grad_key_weight.T, grad_value_weight.T, pair, one)


def solution(mesh):
    whole = Mesh(mesh.devices.reshape(4, 2, 2, 4, 4, 2), (*DP, *TENSOR))
    in_specs = (
        P(DP, TENSOR),
        P(DP, TENSOR),
        P(TENSOR, DP),
        P(TENSOR, DP),
        P(TENSOR, DP),
        P(TENSOR, DP),
        P(DP, TENSOR),
        P(DP, TENSOR),
    )
    out_specs = (P(DP, TENSOR), P(TENSOR, DP), P(TENSOR, DP), P(), P())
    return jax.shard_map(
        per_device, mesh=whole, in_specs=in_specs, out_specs=out_specs, check_vma=False
    )
```

```python
import jax
import jax.numpy as jnp
from jax import lax
from jax.experimental import pallas as pl
from jax.experimental.pallas import tpu as pltpu
from jax.sharding import Mesh, PartitionSpec as P

BLOCK = 128
DP = ("zh", "zm", "zp", "x")
TENSOR = ("y", "c")
RING = ("zh", "zm", "zp")
F32, BF16 = jnp.float32, jnp.bfloat16
VMEM = pl.BlockSpec(memory_space=pltpu.VMEM)
SMEM = pl.BlockSpec(memory_space=pltpu.SMEM)
HBM = pl.BlockSpec(memory_space=pltpu.HBM)


def kernel_call(body, out_shape, in_specs, out_specs=None, scratch=(), flops=0, mib=16):
    if out_specs is None:
        out_specs = jax.tree.map(lambda _: VMEM, out_shape)
    return pl.pallas_call(
        body,
        out_shape=out_shape,
        in_specs=in_specs,
        out_specs=out_specs,
        scratch_shapes=list(scratch),
        cost_estimate=pl.CostEstimate(flops=flops, bytes_accessed=0, transcendentals=0),
        compiler_params=pltpu.CompilerParams(vmem_limit_bytes=mib * 2**20),
    )


def shape(dims, dtype):
    return jax.ShapeDtypeStruct(dims, dtype)


def shift(value, axes, by):
    count = lax.axis_size(axes)
    return lax.ppermute(value, axes, [(i, (i + by) % count) for i in range(count)])


def shift_by_core(value, axes, by):
    count = lax.axis_size(axes)
    pairs = [
        (i * 2 + core, (i + (by, -by)[core]) % count * 2 + core)
        for i in range(count)
        for core in range(2)
    ]
    return lax.ppermute(value, (*axes, "c"), pairs)


def spread(block, axes):
    count = lax.axis_size(axes)
    copies = jnp.broadcast_to(block[None], (count, *block.shape))
    return lax.all_to_all(copies, axes, 0, 0, tiled=True)


def grads_body(key_ref, value_ref, out_ref, key, value, sems):
    copies = [
        pltpu.make_async_copy(source, target, sems.at[i])
        for i, (source, target) in enumerate(((key_ref, key), (value_ref, value)))
    ]
    for copy in copies:
        copy.start()
    for copy in copies:
        copy.wait()
    key, value = key[...].T, value[...].T
    for x in range(4):
        rows = []
        for zz in range(2):
            start = zz * 64 + x * 16
            rows += [key[start : start + 16], value[start : start + 16]]
        block = jnp.concatenate(rows, axis=0)
        for copy in range(4):
            out_ref[x, copy] = block


def scale_body(x_ref, x_scale_ref, key_ref, key_scale_ref, value_ref, value_scale_ref, out_ref, weight_ref):
    x_scale = x_scale_ref[...].T
    scales = (key_scale_ref[...].T, value_scale_ref[...].T)
    for b in range(8):
        at = slice(b * BLOCK, (b + 1) * BLOCK)
        out_ref[:, at] = (x_ref[:, at].astype(F32) * x_scale[:, b : b + 1]).astype(BF16)
        for part, ref in enumerate((key_ref, value_ref)):
            scaled = (ref[:, at].astype(F32) * scales[part][:, b : b + 1]).astype(BF16)
            for copy in range(4):
                weight_ref[copy, part * 16 : (part + 1) * 16, at] = scaled


def weight_body(place, own, twin, x0, x1, x2, x3, keep_ref, key_ref, value_ref, total):
    x, zp, core = place[0], place[2], place[3]
    members = [lax.rem(x + k, 4) for k in (0, 3 - 2 * core, 2, 1 + 2 * core)]
    inputs = jnp.concatenate([ref[...] for ref in (x0, x1, x2, x3)], axis=0)
    for i, part in enumerate((own, twin)):
        lhs = jnp.concatenate([part[member] for member in members], axis=1)
        value = jnp.dot(lhs, inputs, preferred_element_type=F32)
        total[i] = value.reshape(4, 2, 32, 1024)
        zm = lax.rem(core + i, 2)
        for zh in range(4):
            keep_ref[zh, zm] = total[i, zh, zp]
            key_ref[zh, zm] = total[i, zh, 1 - zp, :16].astype(BF16)
            value_ref[zh, zm] = total[i, zh, 1 - zp, 16:].astype(BF16)


def input_body(place, own, twin, w0, w1, w2, w3, keep_ref, out1, out2, out3, weight):
    x, zl, core = place[0], place[1] * 2 + place[2], place[3]
    for k, ref in ((0, w0), (3 - 2 * core, w1), (2, w2), (1 + 2 * core, w3)):
        group = lax.rem(zl + k, 4)
        half, zp = lax.rem(group // 2 + core, 2), lax.rem(group, 2)
        for zh in range(4):
            weight[half, zh, zp] = ref[zh]
    for k, out in ((0, keep_ref), (1 + 2 * core, out1), (2, out2), (3 - 2 * core, out3)):
        member = lax.rem(x + k, 4)
        lhs = jnp.concatenate([own[member].T, twin[member].T], axis=1)
        out[...] = jnp.dot(
            lhs, weight[...].reshape(512, 1024), preferred_element_type=F32
        ).astype(out.dtype)


def near_body(keep_ref, key_ref, value_ref, out_ref):
    for zh in range(4):
        for zm in range(2):
            keep = keep_ref[zh, zm]
            out_ref[zh * 2 + zm, :16] = (keep[:16] + key_ref[zh, zm].astype(F32)).astype(BF16)
            out_ref[zh * 2 + zm, 16:] = (keep[16:] + value_ref[zh, zm].astype(F32)).astype(BF16)


def peak_body(far_ref, keep_ref, r1, r2, r3, weight_ref, input_ref, peak_ref):
    weight = far_ref[0].astype(F32)
    for i in range(1, 8):
        weight = weight + far_ref[i].astype(F32)
    weight_ref[...] = weight
    total = keep_ref[...] + r1[...].astype(F32) + r2[...].astype(F32) + r3[...].astype(F32)
    input_ref[...] = total
    input_peak = jnp.max(jnp.abs(total))
    size = jnp.abs(weight)
    lane = lax.broadcasted_iota(jnp.int32, peak_ref.shape, 1)
    peak_ref[...] = jnp.where(
        lane == 0,
        jnp.max(size[:16]),
        jnp.where(lane == 1, jnp.max(size[16:]), input_peak),
    )


def final_body(peaks_ref, weight_ref, input_ref, out_ref, key_ref, value_ref, pair_ref, one_ref):
    peaks = jnp.max(peaks_ref[...], axis=0, keepdims=True) + 1e-06
    key_peak, value_peak, input_peak = peaks[0, 0], peaks[0, 1], peaks[0, 2]
    key_ref[...] = (weight_ref[:16] / key_peak).astype(BF16)
    value_ref[...] = (weight_ref[16:] / value_peak).astype(BF16)
    out_ref[...] = (input_ref[...] / input_peak).astype(BF16)
    pair_ref[0] = key_peak
    pair_ref[1] = value_peak
    one_ref[0] = input_peak


def per_device(
    x_quant, x_scale, key_quant, key_scale, value_quant, value_scale, grad_key, grad_value
):
    place = jnp.stack([lax.axis_index(axis) for axis in ("x", "zm", "zp", "c")]).astype(jnp.int32)

    own = kernel_call(
        grads_body,
        shape((4, 4, 64, 192), BF16),
        [HBM] * 2,
        scratch=[pltpu.VMEM((192, 128), BF16)] * 2 + [pltpu.SemaphoreType.DMA((2,))],
        mib=60,
    )(grad_key, grad_value)
    own = lax.all_to_all(own.reshape(16, 64, 192), ("x", "y"), 0, 0, tiled=True)
    own = own.reshape(4, 256, 192)
    twin = lax.ppermute(own, "c", [(0, 1), (1, 0)])

    inputs, weight = kernel_call(
        scale_body, (shape((192, 1024), BF16), shape((4, 32, 1024), BF16)), [VMEM] * 6
    )(x_quant, x_scale.T, key_quant.T, key_scale, value_quant.T, value_scale)
    line = ("x",)
    others = [
        shift_by_core(inputs, line, 1),
        shift(inputs, "x", 2),
        shift_by_core(inputs, line, -1),
    ]

    own, weight = lax.optimization_barrier((own, weight))
    weight = lax.all_to_all(weight, "zh", 0, 0, tiled=True)

    keep, key, value = kernel_call(
        weight_body,
        (shape((4, 2, 32, 1024), F32),) + (shape((4, 2, 16, 1024), BF16),) * 2,
        [SMEM] + [VMEM] * 6,
        scratch=[pltpu.VMEM((2, 4, 2, 32, 1024), F32)],
        flops=10**11,
    )(place, own, twin, inputs, *others)
    key, value = shift_by_core(key, RING, -1), shift_by_core(value, RING, 1)
    weights = [weight] + [shift_by_core(weight, RING, by) for by in (1, 2, -1)]
    part = kernel_call(near_body, shape((8, 32, 1024), BF16), [VMEM] * 3)(keep, key, value)
    far = lax.all_to_all(part, ("zh", "zm"), 0, 0, tiled=True)

    keep, ahead, across, behind = kernel_call(
        input_body,
        (shape((192, 1024), F32),) + (shape((192, 1024), BF16),) * 3,
        [SMEM] + [VMEM] * 6,
        scratch=[pltpu.VMEM((2, 4, 2, 32, 1024), BF16)],
        flops=10**11,
    )(place, own, twin, *weights)
    parts = [
        shift_by_core(ahead, line, 1),
        shift(across, "x", 2),
        shift_by_core(behind, line, -1),
    ]

    weight_sum, input_sum, peaks = kernel_call(
        peak_body,
        (shape((32, 1024), F32), shape((192, 1024), F32), shape((32, 128), F32)),
        [VMEM] * 5,
    )(far, keep, *parts)
    peaks = lax.all_to_all(peaks, ("x", *TENSOR), 0, 0, tiled=True)
    peaks = spread(jnp.max(peaks, axis=0), RING)
    grad_input, grad_key_weight, grad_value_weight, pair, one = kernel_call(
        final_body,
        (
            shape((192, 1024), BF16),
            shape((16, 1024), BF16),
            shape((16, 1024), BF16),
            shape((2,), F32),
            shape((1,), F32),
        ),
        [VMEM] * 3,
        (VMEM, VMEM, VMEM, SMEM, SMEM),
    )(peaks.reshape(16, 128), weight_sum, input_sum)
    return (grad_input, grad_key_weight.T, grad_value_weight.T, pair, one)


def solution(mesh):
    whole = Mesh(mesh.devices.reshape(4, 2, 2, 4, 4, 2), (*DP, *TENSOR))
    in_specs = (
        P(DP, TENSOR),
        P(DP, TENSOR),
        P(TENSOR, DP),
        P(TENSOR, DP),
        P(TENSOR, DP),
        P(TENSOR, DP),
        P(DP, TENSOR),
        P(DP, TENSOR),
    )
    out_specs = (P(DP, TENSOR), P(TENSOR, DP), P(TENSOR, DP), P(), P())
    return jax.shard_map(
        per_device, mesh=whole, in_specs=in_specs, out_specs=out_specs, check_vma=False
    )
```

```python
import jax
import jax.numpy as jnp
from jax import lax
from jax.experimental import pallas as pl
from jax.experimental.pallas import tpu as pltpu
from jax.sharding import Mesh, PartitionSpec as P

BLOCK = 128
DP = ("zh", "zm", "zp", "x")
TENSOR = ("y", "c")
RING = ("zh", "zm", "zp")
F32, BF16 = jnp.float32, jnp.bfloat16
VMEM = pl.BlockSpec(memory_space=pltpu.VMEM)
SMEM = pl.BlockSpec(memory_space=pltpu.SMEM)
HBM = pl.BlockSpec(memory_space=pltpu.HBM)


def kernel_call(body, out_shape, in_specs, out_specs=None, scratch=(), flops=0, mib=16):
    if out_specs is None:
        out_specs = jax.tree.map(lambda _: VMEM, out_shape)
    return pl.pallas_call(
        body,
        out_shape=out_shape,
        in_specs=in_specs,
        out_specs=out_specs,
        scratch_shapes=list(scratch),
        cost_estimate=pl.CostEstimate(flops=flops, bytes_accessed=0, transcendentals=0),
        compiler_params=pltpu.CompilerParams(vmem_limit_bytes=mib * 2**20),
    )


def shape(dims, dtype):
    return jax.ShapeDtypeStruct(dims, dtype)


def shift(value, axes, by):
    count = lax.axis_size(axes)
    return lax.ppermute(value, axes, [(i, (i + by) % count) for i in range(count)])


def shift_by_core(value, axes, by):
    count = lax.axis_size(axes)
    pairs = [
        (i * 2 + core, (i + (by, -by)[core]) % count * 2 + core)
        for i in range(count)
        for core in range(2)
    ]
    return lax.ppermute(value, (*axes, "c"), pairs)


def spread(block, axes):
    count = lax.axis_size(axes)
    copies = jnp.broadcast_to(block[None], (count, *block.shape))
    return lax.all_to_all(copies, axes, 0, 0, tiled=True)


def prepare_body(*refs):
    sources, (grads_ref, out_ref, weight_ref) = refs[:8], refs[8:11]
    targets, sems = refs[11:19], refs[19]
    copies = [
        pltpu.make_async_copy(source, target, sems.at[i])
        for i, (source, target) in enumerate(zip(sources, targets))
    ]
    for copy in copies:
        copy.start()
    for copy in copies:
        copy.wait()
    grad_key, grad_value, x_ref, x_scale_ref, key_ref, key_scale_ref, value_ref, value_scale_ref = targets
    key, value = grad_key[...].T, grad_value[...].T
    for x in range(4):
        rows = []
        for zz in range(2):
            start = zz * 64 + x * 16
            rows += [key[start : start + 16], value[start : start + 16]]
        block = jnp.concatenate(rows, axis=0)
        for copy in range(4):
            grads_ref[x, copy] = block
    x_scale = x_scale_ref[...].T
    scales = (key_scale_ref[...].T, value_scale_ref[...].T)
    for b in range(8):
        at = slice(b * BLOCK, (b + 1) * BLOCK)
        out_ref[:, at] = (x_ref[:, at].astype(F32) * x_scale[:, b : b + 1]).astype(BF16)
        for part, ref in enumerate((key_ref, value_ref)):
            scaled = (ref[:, at].astype(F32) * scales[part][:, b : b + 1]).astype(BF16)
            for copy in range(4):
                weight_ref[copy, part * 16 : (part + 1) * 16, at] = scaled


def weight_body(place, own, twin, x0, x1, x2, x3, keep_ref, key_ref, value_ref, total):
    x, zp, core = place[0], place[2], place[3]
    members = [lax.rem(x + k, 4) for k in (0, 3 - 2 * core, 2, 1 + 2 * core)]
    inputs = jnp.concatenate([ref[...] for ref in (x0, x1, x2, x3)], axis=0)
    for i, part in enumerate((own, twin)):
        lhs = jnp.concatenate([part[member] for member in members], axis=1)
        value = jnp.dot(lhs, inputs, preferred_element_type=F32)
        total[i] = value.reshape(4, 2, 32, 1024)
        zm = lax.rem(core + i, 2)
        for zh in range(4):
            keep_ref[zh, zm] = total[i, zh, zp]
            key_ref[zh, zm] = total[i, zh, 1 - zp, :16].astype(BF16)
            value_ref[zh, zm] = total[i, zh, 1 - zp, 16:].astype(BF16)


def input_body(place, own, twin, w0, w1, w2, w3, keep_ref, out1, out2, out3, weight):
    x, zl, core = place[0], place[1] * 2 + place[2], place[3]
    for k, ref in ((0, w0), (3 - 2 * core, w1), (2, w2), (1 + 2 * core, w3)):
        group = lax.rem(zl + k, 4)
        half, zp = lax.rem(group // 2 + core, 2), lax.rem(group, 2)
        for zh in range(4):
            weight[half, zh, zp] = ref[zh]
    for k, out in ((0, keep_ref), (1 + 2 * core, out1), (2, out2), (3 - 2 * core, out3)):
        member = lax.rem(x + k, 4)
        lhs = jnp.concatenate([own[member].T, twin[member].T], axis=1)
        out[...] = jnp.dot(
            lhs, weight[...].reshape(512, 1024), preferred_element_type=F32
        ).astype(out.dtype)


def near_body(keep_ref, key_ref, value_ref, out_ref):
    for zh in range(4):
        for zm in range(2):
            keep = keep_ref[zh, zm]
            out_ref[zh * 2 + zm, :16] = (keep[:16] + key_ref[zh, zm].astype(F32)).astype(BF16)
            out_ref[zh * 2 + zm, 16:] = (keep[16:] + value_ref[zh, zm].astype(F32)).astype(BF16)


def peak_body(far_ref, keep_ref, r1, r2, r3, weight_ref, input_ref, peak_ref):
    weight = far_ref[0].astype(F32)
    for i in range(1, 8):
        weight = weight + far_ref[i].astype(F32)
    weight_ref[...] = weight
    total = keep_ref[...] + r1[...].astype(F32) + r2[...].astype(F32) + r3[...].astype(F32)
    input_ref[...] = total
    input_peak = jnp.max(jnp.abs(total))
    size = jnp.abs(weight)
    lane = lax.broadcasted_iota(jnp.int32, peak_ref.shape, 1)
    peak_ref[...] = jnp.where(
        lane == 0,
        jnp.max(size[:16]),
        jnp.where(lane == 1, jnp.max(size[16:]), input_peak),
    )


def final_body(peaks_ref, weight_ref, input_ref, out_ref, key_ref, value_ref, pair_ref, one_ref):
    peaks = jnp.max(peaks_ref[...], axis=0, keepdims=True) + 1e-06
    key_peak, value_peak, input_peak = peaks[0, 0], peaks[0, 1], peaks[0, 2]
    key_ref[...] = (weight_ref[:16] / key_peak).astype(BF16)
    value_ref[...] = (weight_ref[16:] / value_peak).astype(BF16)
    out_ref[...] = (input_ref[...] / input_peak).astype(BF16)
    pair_ref[0] = key_peak
    pair_ref[1] = value_peak
    one_ref[0] = input_peak


def per_device(
    x_quant, x_scale, key_quant, key_scale, value_quant, value_scale, grad_key, grad_value
):
    place = jnp.stack([lax.axis_index(axis) for axis in ("x", "zm", "zp", "c")]).astype(jnp.int32)

    operands = (
        grad_key, grad_value, x_quant, x_scale.T, key_quant.T, key_scale, value_quant.T, value_scale
    )
    own, inputs, weight = kernel_call(
        prepare_body,
        (shape((4, 4, 64, 192), BF16), shape((192, 1024), BF16), shape((4, 32, 1024), BF16)),
        [HBM] * 8,
        scratch=[pltpu.VMEM(operand.shape, operand.dtype) for operand in operands]
        + [pltpu.SemaphoreType.DMA((8,))],
        mib=60,
    )(*operands)

    own = lax.all_to_all(own.reshape(16, 64, 192), ("x", "y"), 0, 0, tiled=True)
    own = own.reshape(4, 256, 192)
    twin = lax.ppermute(own, "c", [(0, 1), (1, 0)])

    line = ("x",)
    others = [
        shift_by_core(inputs, line, 1),
        shift(inputs, "x", 2),
        shift_by_core(inputs, line, -1),
    ]

    own, weight = lax.optimization_barrier((own, weight))
    weight = lax.all_to_all(weight, "zh", 0, 0, tiled=True)

    keep, key, value = kernel_call(
        weight_body,
        (shape((4, 2, 32, 1024), F32),) + (shape((4, 2, 16, 1024), BF16),) * 2,
        [SMEM] + [VMEM] * 6,
        scratch=[pltpu.VMEM((2, 4, 2, 32, 1024), F32)],
        flops=10**11,
    )(place, own, twin, inputs, *others)
    key, value = shift_by_core(key, RING, -1), shift_by_core(value, RING, 1)
    weights = [weight] + [shift_by_core(weight, RING, by) for by in (1, 2, -1)]
    part = kernel_call(near_body, shape((8, 32, 1024), BF16), [VMEM] * 3)(keep, key, value)
    far = lax.all_to_all(part, ("zh", "zm"), 0, 0, tiled=True)

    keep, ahead, across, behind = kernel_call(
        input_body,
        (shape((192, 1024), F32),) + (shape((192, 1024), BF16),) * 3,
        [SMEM] + [VMEM] * 6,
        scratch=[pltpu.VMEM((2, 4, 2, 32, 1024), BF16)],
        flops=10**11,
    )(place, own, twin, *weights)
    parts = [
        shift_by_core(ahead, line, 1),
        shift(across, "x", 2),
        shift_by_core(behind, line, -1),
    ]

    weight_sum, input_sum, peaks = kernel_call(
        peak_body,
        (shape((32, 1024), F32), shape((192, 1024), F32), shape((32, 128), F32)),
        [VMEM] * 5,
    )(far, keep, *parts)
    peaks = lax.all_to_all(peaks, ("x", *TENSOR), 0, 0, tiled=True)
    peaks = spread(jnp.max(peaks, axis=0), RING)
    grad_input, grad_key_weight, grad_value_weight, pair, one = kernel_call(
        final_body,
        (
            shape((192, 1024), BF16),
            shape((16, 1024), BF16),
            shape((16, 1024), BF16),
            shape((2,), F32),
            shape((1,), F32),
        ),
        [VMEM] * 3,
        (VMEM, VMEM, VMEM, SMEM, SMEM),
    )(peaks.reshape(16, 128), weight_sum, input_sum)
    return (grad_input, grad_key_weight.T, grad_value_weight.T, pair, one)


def solution(mesh):
    whole = Mesh(mesh.devices.reshape(4, 2, 2, 4, 4, 2), (*DP, *TENSOR))
    in_specs = (
        P(DP, TENSOR),
        P(DP, TENSOR),
        P(TENSOR, DP),
        P(TENSOR, DP),
        P(TENSOR, DP),
        P(TENSOR, DP),
        P(DP, TENSOR),
        P(DP, TENSOR),
    )
    out_specs = (P(DP, TENSOR), P(TENSOR, DP), P(TENSOR, DP), P(), P())
    return jax.shard_map(
        per_device, mesh=whole, in_specs=in_specs, out_specs=out_specs, check_vma=False
    )
```

```python
import jax
import jax.numpy as jnp
from jax import lax
from jax.experimental import pallas as pl
from jax.experimental.pallas import tpu as pltpu
from jax.sharding import Mesh, PartitionSpec as P

BLOCK = 128
DP = ("zh", "zm", "zp", "x")
TENSOR = ("y", "c")
RING = ("zh", "zm", "zp")
F32, BF16 = jnp.float32, jnp.bfloat16
VMEM = pl.BlockSpec(memory_space=pltpu.VMEM)
SMEM = pl.BlockSpec(memory_space=pltpu.SMEM)
HBM = pl.BlockSpec(memory_space=pltpu.HBM)


def kernel_call(body, out_shape, in_specs, out_specs=None, scratch=(), flops=0, mib=16):
    if out_specs is None:
        out_specs = jax.tree.map(lambda _: VMEM, out_shape)
    return pl.pallas_call(
        body,
        out_shape=out_shape,
        in_specs=in_specs,
        out_specs=out_specs,
        scratch_shapes=list(scratch),
        cost_estimate=pl.CostEstimate(flops=flops, bytes_accessed=0, transcendentals=0),
        compiler_params=pltpu.CompilerParams(vmem_limit_bytes=mib * 2**20),
    )


def shape(dims, dtype):
    return jax.ShapeDtypeStruct(dims, dtype)


def shift(value, axes, by):
    count = lax.axis_size(axes)
    return lax.ppermute(value, axes, [(i, (i + by) % count) for i in range(count)])


def shift_by_core(value, axes, by):
    count = lax.axis_size(axes)
    pairs = [
        (i * 2 + core, (i + (by, -by)[core]) % count * 2 + core)
        for i in range(count)
        for core in range(2)
    ]
    return lax.ppermute(value, (*axes, "c"), pairs)


def spread(block, axes):
    count = lax.axis_size(axes)
    copies = jnp.broadcast_to(block[None], (count, *block.shape))
    return lax.all_to_all(copies, axes, 0, 0, tiled=True)


def prepare_body(*refs):
    sources, (grads_ref, out_ref, weight_ref) = refs[:8], refs[8:11]
    targets, sems = refs[11:19], refs[19]
    copies = [
        pltpu.make_async_copy(source, target, sems.at[i])
        for i, (source, target) in enumerate(zip(sources, targets))
    ]
    for copy in copies:
        copy.start()
    for copy in copies:
        copy.wait()
    grad_key, grad_value, x_ref, x_scale_ref, key_ref, key_scale_ref, value_ref, value_scale_ref = targets
    key, value = grad_key[...].T, grad_value[...].T
    for x in range(4):
        rows = []
        for zz in range(2):
            start = zz * 64 + x * 16
            rows += [key[start : start + 16], value[start : start + 16]]
        block = jnp.concatenate(rows, axis=0)
        for copy in range(4):
            grads_ref[x, copy] = block
    x_scale = x_scale_ref[...].T
    scales = (key_scale_ref[...].T, value_scale_ref[...].T)
    for b in range(8):
        at = slice(b * BLOCK, (b + 1) * BLOCK)
        out_ref[:, at] = (x_ref[:, at].astype(F32) * x_scale[:, b : b + 1]).astype(BF16)
        for part, ref in enumerate((key_ref, value_ref)):
            scaled = (ref[:, at].astype(F32) * scales[part][:, b : b + 1]).astype(BF16)
            for copy in range(4):
                weight_ref[copy, part * 16 : (part + 1) * 16, at] = scaled


def weight_body(place, own, twin, x0, x1, x2, x3, keep_ref, key_ref, value_ref, total):
    x, zp, core = place[0], place[2], place[3]
    members = [lax.rem(x + k, 4) for k in (0, 3 - 2 * core, 2, 1 + 2 * core)]
    inputs = jnp.concatenate([ref[...] for ref in (x0, x1, x2, x3)], axis=0)
    for i, part in enumerate((own, twin)):
        lhs = jnp.concatenate([part[member] for member in members], axis=1)
        value = jnp.dot(lhs, inputs, preferred_element_type=F32)
        total[i] = value.reshape(4, 2, 32, 1024)
        zm = lax.rem(core + i, 2)
        for zh in range(4):
            keep_ref[zh, zm] = total[i, zh, zp]
            key_ref[zh, zm] = total[i, zh, 1 - zp, :16].astype(BF16)
            value_ref[zh, zm] = total[i, zh, 1 - zp, 16:].astype(BF16)


def input_body(place, own, twin, w0, w1, w2, w3, keep_ref, out1, out2, out3, weight):
    x, zl, core = place[0], place[1] * 2 + place[2], place[3]
    for k, ref in ((0, w0), (3 - 2 * core, w1), (2, w2), (1 + 2 * core, w3)):
        group = lax.rem(zl + k, 4)
        half, zp = lax.rem(group // 2 + core, 2), lax.rem(group, 2)
        for zh in range(4):
            weight[half, zh, zp] = ref[zh]
    for k, out in ((0, keep_ref), (1 + 2 * core, out1), (2, out2), (3 - 2 * core, out3)):
        member = lax.rem(x + k, 4)
        lhs = jnp.concatenate([own[member].T, twin[member].T], axis=1)
        out[...] = jnp.dot(
            lhs, weight[...].reshape(512, 1024), preferred_element_type=F32
        ).astype(out.dtype)


def near_body(keep_ref, key_ref, value_ref, out_ref):
    for zh in range(4):
        for zm in range(2):
            keep = keep_ref[zh, zm]
            out_ref[zh * 2 + zm, :16] = (keep[:16] + key_ref[zh, zm].astype(F32)).astype(BF16)
            out_ref[zh * 2 + zm, 16:] = (keep[16:] + value_ref[zh, zm].astype(F32)).astype(BF16)


def peak_body(far_ref, keep_ref, r1, r2, r3, weight_ref, input_ref, peak_ref):
    weight = far_ref[0].astype(F32)
    for i in range(1, 8):
        weight = weight + far_ref[i].astype(F32)
    weight_ref[...] = weight
    total = keep_ref[...] + r1[...].astype(F32) + r2[...].astype(F32) + r3[...].astype(F32)
    input_ref[...] = total
    input_peak = jnp.max(jnp.abs(total))
    size = jnp.abs(weight)
    lane = lax.broadcasted_iota(jnp.int32, peak_ref.shape, 1)
    peak_ref[...] = jnp.where(
        lane == 0,
        jnp.max(size[:16]),
        jnp.where(lane == 1, jnp.max(size[16:]), input_peak),
    )


def final_body(peaks_ref, weight_ref, input_ref, out_ref, key_ref, value_ref, pair_ref, one_ref):
    peaks = jnp.max(peaks_ref[...], axis=0, keepdims=True) + 1e-06
    key_peak, value_peak, input_peak = peaks[0, 0], peaks[0, 1], peaks[0, 2]
    key_ref[...] = (weight_ref[:16] / key_peak).astype(BF16)
    value_ref[...] = (weight_ref[16:] / value_peak).astype(BF16)
    out_ref[...] = (input_ref[...] / input_peak).astype(BF16)
    pair_ref[0] = key_peak
    pair_ref[1] = value_peak
    one_ref[0] = input_peak


def per_device(
    x_quant, x_scale, key_quant, key_scale, value_quant, value_scale, grad_key, grad_value
):
    place = jnp.stack([lax.axis_index(axis) for axis in ("x", "zm", "zp", "c")]).astype(jnp.int32)

    operands = (
        grad_key, grad_value, x_quant, x_scale.T, key_quant.T, key_scale, value_quant.T, value_scale
    )
    own, inputs, weight = kernel_call(
        prepare_body,
        (shape((4, 4, 64, 192), BF16), shape((192, 1024), BF16), shape((4, 32, 1024), BF16)),
        [HBM] * 8,
        scratch=[pltpu.VMEM(operand.shape, operand.dtype) for operand in operands]
        + [pltpu.SemaphoreType.DMA((8,))],
        mib=60,
    )(*operands)

    own = lax.all_to_all(own.reshape(16, 64, 192), ("x", "y"), 0, 0, tiled=True)
    own = own.reshape(4, 256, 192)
    twin = lax.ppermute(own, "c", [(0, 1), (1, 0)])

    line = ("x",)
    others = [
        shift_by_core(inputs, line, 1),
        shift(inputs, "x", 2),
        shift_by_core(inputs, line, -1),
    ]

    own, weight = lax.optimization_barrier((own, weight))
    weight = lax.all_to_all(weight, "zh", 0, 0, tiled=True)

    keep, key, value = kernel_call(
        weight_body,
        (shape((4, 2, 32, 1024), F32),) + (shape((4, 2, 16, 1024), BF16),) * 2,
        [SMEM] + [VMEM] * 6,
        scratch=[pltpu.VMEM((2, 4, 2, 32, 1024), F32)],
        flops=10**11,
    )(place, own, twin, inputs, *others)
    key, value = shift_by_core(key, RING, -1), shift_by_core(value, RING, 1)
    weights = [weight] + [shift_by_core(weight, RING, by) for by in (1, -2, -1)]
    part = kernel_call(near_body, shape((8, 32, 1024), BF16), [VMEM] * 3)(keep, key, value)
    far = lax.all_to_all(part, ("zh", "zm"), 0, 0, tiled=True)

    keep, ahead, across, behind = kernel_call(
        input_body,
        (shape((192, 1024), F32),) + (shape((192, 1024), BF16),) * 3,
        [SMEM] + [VMEM] * 6,
        scratch=[pltpu.VMEM((2, 4, 2, 32, 1024), BF16)],
        flops=10**11,
    )(place, own, twin, *weights)
    parts = [
        shift_by_core(ahead, line, 1),
        shift(across, "x", 2),
        shift_by_core(behind, line, -1),
    ]

    weight_sum, input_sum, peaks = kernel_call(
        peak_body,
        (shape((32, 1024), F32), shape((192, 1024), F32), shape((32, 128), F32)),
        [VMEM] * 5,
    )(far, keep, *parts)
    peaks = lax.all_to_all(peaks, ("x", *TENSOR), 0, 0, tiled=True)
    peaks = spread(jnp.max(peaks, axis=0), RING)
    grad_input, grad_key_weight, grad_value_weight, pair, one = kernel_call(
        final_body,
        (
            shape((192, 1024), BF16),
            shape((16, 1024), BF16),
            shape((16, 1024), BF16),
            shape((2,), F32),
            shape((1,), F32),
        ),
        [VMEM] * 3,
        (VMEM, VMEM, VMEM, SMEM, SMEM),
    )(peaks.reshape(16, 128), weight_sum, input_sum)
    return (grad_input, grad_key_weight.T, grad_value_weight.T, pair, one)


def solution(mesh):
    whole = Mesh(mesh.devices.reshape(4, 2, 2, 4, 4, 2), (*DP, *TENSOR))
    in_specs = (
        P(DP, TENSOR),
        P(DP, TENSOR),
        P(TENSOR, DP),
        P(TENSOR, DP),
        P(TENSOR, DP),
        P(TENSOR, DP),
        P(DP, TENSOR),
        P(DP, TENSOR),
    )
    out_specs = (P(DP, TENSOR), P(TENSOR, DP), P(TENSOR, DP), P(), P())
    return jax.shard_map(
        per_device, mesh=whole, in_specs=in_specs, out_specs=out_specs, check_vma=False
    )
```

```python
import jax
import jax.numpy as jnp
from jax import lax
from jax.experimental import pallas as pl
from jax.experimental.pallas import tpu as pltpu
from jax.sharding import Mesh, PartitionSpec as P

BLOCK = 128
DP = ("zh", "zm", "zp", "x")
TENSOR = ("y", "c")
RING = ("zh", "zm", "zp")
F32, BF16 = jnp.float32, jnp.bfloat16
VMEM = pl.BlockSpec(memory_space=pltpu.VMEM)
SMEM = pl.BlockSpec(memory_space=pltpu.SMEM)
HBM = pl.BlockSpec(memory_space=pltpu.HBM)


def kernel_call(body, out_shape, in_specs, out_specs=None, scratch=(), flops=0, mib=8):
    if out_specs is None:
        out_specs = jax.tree.map(lambda _: VMEM, out_shape)
    return pl.pallas_call(
        body,
        out_shape=out_shape,
        in_specs=in_specs,
        out_specs=out_specs,
        scratch_shapes=list(scratch),
        cost_estimate=pl.CostEstimate(flops=flops, bytes_accessed=0, transcendentals=0),
        compiler_params=pltpu.CompilerParams(vmem_limit_bytes=mib * 2**20),
    )


def shape(dims, dtype):
    return jax.ShapeDtypeStruct(dims, dtype)


def shift(value, axes, by):
    count = lax.axis_size(axes)
    return lax.ppermute(value, axes, [(i, (i + by) % count) for i in range(count)])


def shift_by_core(value, axes, by):
    count = lax.axis_size(axes)
    pairs = [
        (i * 2 + core, (i + (by, -by)[core]) % count * 2 + core)
        for i in range(count)
        for core in range(2)
    ]
    return lax.ppermute(value, (*axes, "c"), pairs)


def spread(block, axes):
    count = lax.axis_size(axes)
    copies = jnp.broadcast_to(block[None], (count, *block.shape))
    return lax.all_to_all(copies, axes, 0, 0, tiled=True)


def prepare_body(*refs):
    sources, (grads_ref, out_ref, weight_ref) = refs[:8], refs[8:11]
    targets, sems = refs[11:19], refs[19]
    copies = [
        pltpu.make_async_copy(source, target, sems.at[i])
        for i, (source, target) in enumerate(zip(sources, targets))
    ]
    for copy in copies:
        copy.start()
    for copy in copies:
        copy.wait()
    grad_key, grad_value, x_ref, x_scale_ref, key_ref, key_scale_ref, value_ref, value_scale_ref = targets
    key, value = grad_key[...].T, grad_value[...].T
    for x in range(4):
        rows = []
        for zz in range(2):
            start = zz * 64 + x * 16
            rows += [key[start : start + 16], value[start : start + 16]]
        block = jnp.concatenate(rows, axis=0)
        for copy in range(4):
            grads_ref[x, copy] = block
    x_scale = x_scale_ref[...].T
    scales = (key_scale_ref[...].T, value_scale_ref[...].T)
    for b in range(8):
        at = slice(b * BLOCK, (b + 1) * BLOCK)
        out_ref[:, at] = (x_ref[:, at].astype(F32) * x_scale[:, b : b + 1]).astype(BF16)
        for part, ref in enumerate((key_ref, value_ref)):
            scaled = (ref[:, at].astype(F32) * scales[part][:, b : b + 1]).astype(BF16)
            for copy in range(4):
                weight_ref[copy, part * 16 : (part + 1) * 16, at] = scaled


def weight_body(place, own, twin, x0, x1, x2, x3, keep_ref, key_ref, value_ref):
    x, zp, core = place[0], place[2], place[3]
    members = [lax.rem(x + k, 4) for k in (0, 3 - 2 * core, 2, 1 + 2 * core)]
    inputs = jnp.concatenate([ref[...] for ref in (x0, x1, x2, x3)], axis=0)
    for i, part in enumerate((own, twin)):
        lhs = jnp.concatenate([part[member] for member in members], axis=1)
        value = jnp.dot(lhs, inputs, preferred_element_type=F32)
        value = value.reshape(4, 2, 32, 1024)
        zm = lax.rem(core + i, 2)
        for zh in range(4):
            keep_ref[zh, zm] = jnp.where(zp == 0, value[zh, 0], value[zh, 1])
            away = jnp.where(zp == 0, value[zh, 1], value[zh, 0]).astype(BF16)
            key_ref[zh, zm] = away[:16]
            value_ref[zh, zm] = away[16:]


def input_body(place, own, twin, w0, w1, w2, w3, keep_ref, out1, out2, out3, weight):
    x, zl, core = place[0], place[1] * 2 + place[2], place[3]
    for k, ref in ((0, w0), (3 - 2 * core, w1), (2, w2), (1 + 2 * core, w3)):
        group = lax.rem(zl + k, 4)
        half, zp = lax.rem(group // 2 + core, 2), lax.rem(group, 2)
        for zh in range(4):
            weight[half, zh, zp] = ref[zh]
    for k, out in ((0, keep_ref), (1 + 2 * core, out1), (2, out2), (3 - 2 * core, out3)):
        member = lax.rem(x + k, 4)
        lhs = jnp.concatenate([own[member].T, twin[member].T], axis=1)
        out[...] = jnp.dot(
            lhs, weight[...].reshape(512, 1024), preferred_element_type=F32
        ).astype(out.dtype)


def near_body(keep_ref, key_ref, value_ref, out_ref):
    for zh in range(4):
        for zm in range(2):
            keep = keep_ref[zh, zm]
            out_ref[zh * 2 + zm, :16] = (keep[:16] + key_ref[zh, zm].astype(F32)).astype(BF16)
            out_ref[zh * 2 + zm, 16:] = (keep[16:] + value_ref[zh, zm].astype(F32)).astype(BF16)


def peak_body(far_ref, keep_ref, r1, r2, r3, weight_ref, input_ref, peak_ref):
    weight = far_ref[0].astype(F32)
    for i in range(1, 8):
        weight = weight + far_ref[i].astype(F32)
    weight_ref[...] = weight
    total = keep_ref[...] + r1[...].astype(F32) + r2[...].astype(F32) + r3[...].astype(F32)
    input_ref[...] = total
    input_peak = jnp.max(jnp.abs(total))
    size = jnp.abs(weight)
    lane = lax.broadcasted_iota(jnp.int32, peak_ref.shape, 1)
    peak_ref[...] = jnp.where(
        lane == 0,
        jnp.max(size[:16]),
        jnp.where(lane == 1, jnp.max(size[16:]), input_peak),
    )


def final_body(peaks_ref, weight_ref, input_ref, out_ref, key_ref, value_ref, pair_ref, one_ref):
    peaks = jnp.max(peaks_ref[...], axis=0, keepdims=True) + 1e-06
    key_peak, value_peak, input_peak = peaks[0, 0], peaks[0, 1], peaks[0, 2]
    key_ref[...] = (weight_ref[:16] / key_peak).astype(BF16)
    value_ref[...] = (weight_ref[16:] / value_peak).astype(BF16)
    out_ref[...] = (input_ref[...] / input_peak).astype(BF16)
    pair_ref[0] = key_peak
    pair_ref[1] = value_peak
    one_ref[0] = input_peak


def per_device(
    x_quant, x_scale, key_quant, key_scale, value_quant, value_scale, grad_key, grad_value
):
    place = jnp.stack([lax.axis_index(axis) for axis in ("x", "zm", "zp", "c")]).astype(jnp.int32)

    operands = (
        grad_key, grad_value, x_quant, x_scale.T, key_quant.T, key_scale, value_quant.T, value_scale
    )
    own, inputs, weight = kernel_call(
        prepare_body,
        (shape((4, 4, 64, 192), BF16), shape((192, 1024), BF16), shape((4, 32, 1024), BF16)),
        [HBM] * 8,
        scratch=[pltpu.VMEM(operand.shape, operand.dtype) for operand in operands]
        + [pltpu.SemaphoreType.DMA((8,))],
        mib=60,
    )(*operands)

    own = lax.all_to_all(own.reshape(16, 64, 192), ("x", "y"), 0, 0, tiled=True)
    own = own.reshape(4, 256, 192)
    twin = lax.ppermute(own, "c", [(0, 1), (1, 0)])

    line = ("x",)
    others = [
        shift_by_core(inputs, line, 1),
        shift(inputs, "x", 2),
        shift_by_core(inputs, line, -1),
    ]

    own, weight = lax.optimization_barrier((own, weight))
    weight = lax.all_to_all(weight, "zh", 0, 0, tiled=True)

    keep, key, value = kernel_call(
        weight_body,
        (shape((4, 2, 32, 1024), F32),) + (shape((4, 2, 16, 1024), BF16),) * 2,
        [SMEM] + [VMEM] * 6,
        flops=10**11,
    )(place, own, twin, inputs, *others)
    key, value = shift_by_core(key, RING, -1), shift_by_core(value, RING, 1)
    weights = [weight] + [shift_by_core(weight, RING, by) for by in (1, -2, -1)]
    part = kernel_call(near_body, shape((8, 32, 1024), BF16), [VMEM] * 3)(keep, key, value)
    far = lax.all_to_all(part, ("zh", "zm"), 0, 0, tiled=True)

    keep, ahead, across, behind = kernel_call(
        input_body,
        (shape((192, 1024), F32),) + (shape((192, 1024), BF16),) * 3,
        [SMEM] + [VMEM] * 6,
        scratch=[pltpu.VMEM((2, 4, 2, 32, 1024), BF16)],
        flops=10**11,
    )(place, own, twin, *weights)
    parts = [
        shift_by_core(ahead, line, 1),
        shift(across, "x", 2),
        shift_by_core(behind, line, -1),
    ]

    weight_sum, input_sum, peaks = kernel_call(
        peak_body,
        (shape((32, 1024), F32), shape((192, 1024), F32), shape((32, 128), F32)),
        [VMEM] * 5,
    )(far, keep, *parts)
    peaks = lax.all_to_all(peaks, ("x", *TENSOR), 0, 0, tiled=True)
    peaks = spread(jnp.max(peaks, axis=0), RING)
    grad_input, grad_key_weight, grad_value_weight, pair, one = kernel_call(
        final_body,
        (
            shape((192, 1024), BF16),
            shape((16, 1024), BF16),
            shape((16, 1024), BF16),
            shape((2,), F32),
            shape((1,), F32),
        ),
        [VMEM] * 3,
        (VMEM, VMEM, VMEM, SMEM, SMEM),
    )(peaks.reshape(16, 128), weight_sum, input_sum)
    return (grad_input, grad_key_weight.T, grad_value_weight.T, pair, one)


def solution(mesh):
    whole = Mesh(mesh.devices.reshape(4, 2, 2, 4, 4, 2), (*DP, *TENSOR))
    in_specs = (
        P(DP, TENSOR),
        P(DP, TENSOR),
        P(TENSOR, DP),
        P(TENSOR, DP),
        P(TENSOR, DP),
        P(TENSOR, DP),
        P(DP, TENSOR),
        P(DP, TENSOR),
    )
    out_specs = (P(DP, TENSOR), P(TENSOR, DP), P(TENSOR, DP), P(), P())
    return jax.shard_map(
        per_device, mesh=whole, in_specs=in_specs, out_specs=out_specs, check_vma=False
    )
```

```python
import jax
import jax.numpy as jnp
from jax import lax
from jax.experimental import pallas as pl
from jax.experimental.pallas import tpu as pltpu
from jax.sharding import Mesh, PartitionSpec as P

BLOCK = 128
DP = ("zh", "zm", "zp", "x")
TENSOR = ("y", "c")
RING = ("zh", "zm", "zp")
F32, BF16 = jnp.float32, jnp.bfloat16
VMEM = pl.BlockSpec(memory_space=pltpu.VMEM)
SMEM = pl.BlockSpec(memory_space=pltpu.SMEM)
HBM = pl.BlockSpec(memory_space=pltpu.HBM)


def kernel_call(body, out_shape, in_specs, out_specs=None, scratch=(), flops=0, mib=16):
    if out_specs is None:
        out_specs = jax.tree.map(lambda _: VMEM, out_shape)
    return pl.pallas_call(
        body,
        out_shape=out_shape,
        in_specs=in_specs,
        out_specs=out_specs,
        scratch_shapes=list(scratch),
        cost_estimate=pl.CostEstimate(flops=flops, bytes_accessed=0, transcendentals=0),
        compiler_params=pltpu.CompilerParams(vmem_limit_bytes=mib * 2**20),
    )


def shape(dims, dtype):
    return jax.ShapeDtypeStruct(dims, dtype)


def shift(value, axes, by):
    count = lax.axis_size(axes)
    return lax.ppermute(value, axes, [(i, (i + by) % count) for i in range(count)])


def shift_by_core(value, axes, by):
    count = lax.axis_size(axes)
    pairs = [
        (i * 2 + core, (i + (by, -by)[core]) % count * 2 + core)
        for i in range(count)
        for core in range(2)
    ]
    return lax.ppermute(value, (*axes, "c"), pairs)


def spread(block, axes):
    count = lax.axis_size(axes)
    copies = jnp.broadcast_to(block[None], (count, *block.shape))
    return lax.all_to_all(copies, axes, 0, 0, tiled=True)


def prepare_body(*refs):
    sources, (grads_ref, out_ref, weight_ref) = refs[:8], refs[8:11]
    targets, sems = refs[11:19], refs[19]
    copies = [
        pltpu.make_async_copy(source, target, sems.at[i])
        for i, (source, target) in enumerate(zip(sources, targets))
    ]
    for copy in copies:
        copy.start()
    for copy in copies:
        copy.wait()
    grad_key, grad_value, x_ref, x_scale_ref, key_ref, key_scale_ref, value_ref, value_scale_ref = targets
    key, value = grad_key[...].T, grad_value[...].T
    for x in range(4):
        rows = []
        for zz in range(2):
            start = zz * 64 + x * 16
            rows += [key[start : start + 16], value[start : start + 16]]
        block = jnp.concatenate(rows, axis=0)
        for copy in range(4):
            grads_ref[x, copy] = block
    x_scale = x_scale_ref[...].T
    scales = (key_scale_ref[...].T, value_scale_ref[...].T)
    for b in range(8):
        at = slice(b * BLOCK, (b + 1) * BLOCK)
        out_ref[:, at] = (x_ref[:, at].astype(F32) * x_scale[:, b : b + 1]).astype(BF16)
        for part, ref in enumerate((key_ref, value_ref)):
            scaled = (ref[:, at].astype(F32) * scales[part][:, b : b + 1]).astype(BF16)
            for copy in range(4):
                weight_ref[copy, part * 16 : (part + 1) * 16, at] = scaled


def weight_body(place, own, twin, x0, x1, x2, x3, keep_ref, key_ref, value_ref, total):
    x, zp, core = place[0], place[2], place[3]
    members = [lax.rem(x + k, 4) for k in (0, 3 - 2 * core, 2, 1 + 2 * core)]
    inputs = jnp.concatenate([ref[...] for ref in (x0, x1, x2, x3)], axis=0)
    for i, part in enumerate((own, twin)):
        lhs = jnp.concatenate([part[member] for member in members], axis=1)
        value = jnp.dot(lhs, inputs, preferred_element_type=F32)
        total[i] = value.reshape(4, 2, 32, 1024)
        zm = lax.rem(core + i, 2)
        for zh in range(4):
            keep_ref[zh, zm] = total[i, zh, zp]
            key_ref[zh, zm] = total[i, zh, 1 - zp, :16].astype(BF16)
            value_ref[zh, zm] = total[i, zh, 1 - zp, 16:].astype(BF16)


def input_body(place, own, twin, w0, w1, w2, w3, keep_ref, out1, out2, out3, weight):
    x, zl, core = place[0], place[1] * 2 + place[2], place[3]
    for k, ref in ((0, w0), (1 + 2 * core, w1), (2, w2), (3 - 2 * core, w3)):
        group = lax.rem(zl + k, 4)
        half, zp = lax.rem(group // 2 + core, 2), lax.rem(group, 2)
        for zh in range(4):
            weight[half, zh, zp] = ref[zh]
    for k, out in ((0, keep_ref), (1 + 2 * core, out1), (2, out2), (3 - 2 * core, out3)):
        member = lax.rem(x + k, 4)
        lhs = jnp.concatenate([own[member].T, twin[member].T], axis=1)
        out[...] = jnp.dot(
            lhs, weight[...].reshape(512, 1024), preferred_element_type=F32
        ).astype(out.dtype)


def near_body(keep_ref, key_ref, value_ref, out_ref):
    for zh in range(4):
        for zm in range(2):
            keep = keep_ref[zh, zm]
            out_ref[zh * 2 + zm, :16] = (keep[:16] + key_ref[zh, zm].astype(F32)).astype(BF16)
            out_ref[zh * 2 + zm, 16:] = (keep[16:] + value_ref[zh, zm].astype(F32)).astype(BF16)


def peak_body(far_ref, keep_ref, r1, r2, r3, weight_ref, input_ref, peak_ref):
    weight = far_ref[0].astype(F32)
    for i in range(1, 8):
        weight = weight + far_ref[i].astype(F32)
    weight_ref[...] = weight
    total = keep_ref[...] + r1[...].astype(F32) + r2[...].astype(F32) + r3[...].astype(F32)
    input_ref[...] = total
    input_peak = jnp.max(jnp.abs(total))
    size = jnp.abs(weight)
    lane = lax.broadcasted_iota(jnp.int32, peak_ref.shape, 1)
    peak_ref[...] = jnp.where(
        lane == 0,
        jnp.max(size[:16]),
        jnp.where(lane == 1, jnp.max(size[16:]), input_peak),
    )


def final_body(peaks_ref, weight_ref, input_ref, out_ref, key_ref, value_ref, pair_ref, one_ref):
    peaks = jnp.max(peaks_ref[...], axis=0, keepdims=True) + 1e-06
    key_peak, value_peak, input_peak = peaks[0, 0], peaks[0, 1], peaks[0, 2]
    key_ref[...] = (weight_ref[:16] / key_peak).astype(BF16)
    value_ref[...] = (weight_ref[16:] / value_peak).astype(BF16)
    out_ref[...] = (input_ref[...] / input_peak).astype(BF16)
    pair_ref[0] = key_peak
    pair_ref[1] = value_peak
    one_ref[0] = input_peak


def per_device(
    x_quant, x_scale, key_quant, key_scale, value_quant, value_scale, grad_key, grad_value
):
    place = jnp.stack([lax.axis_index(axis) for axis in ("x", "zm", "zp", "c")]).astype(jnp.int32)

    operands = (
        grad_key, grad_value, x_quant, x_scale.T, key_quant.T, key_scale, value_quant.T, value_scale
    )
    own, inputs, weight = kernel_call(
        prepare_body,
        (shape((4, 4, 64, 192), BF16), shape((192, 1024), BF16), shape((4, 32, 1024), BF16)),
        [HBM] * 8,
        scratch=[pltpu.VMEM(operand.shape, operand.dtype) for operand in operands]
        + [pltpu.SemaphoreType.DMA((8,))],
        mib=60,
    )(*operands)

    own = lax.all_to_all(own.reshape(16, 64, 192), ("x", "y"), 0, 0, tiled=True)
    own = own.reshape(4, 256, 192)
    twin = lax.ppermute(own, "c", [(0, 1), (1, 0)])

    line = ("x",)
    others = [
        shift_by_core(inputs, line, 1),
        shift(inputs, "x", 2),
        shift_by_core(inputs, line, -1),
    ]

    own, weight = lax.optimization_barrier((own, weight))
    weight = lax.all_to_all(weight, "zh", 0, 0, tiled=True)

    keep, key, value = kernel_call(
        weight_body,
        (shape((4, 2, 32, 1024), F32),) + (shape((4, 2, 16, 1024), BF16),) * 2,
        [SMEM] + [VMEM] * 6,
        scratch=[pltpu.VMEM((2, 4, 2, 32, 1024), F32)],
        flops=10**11,
    )(place, own, twin, inputs, *others)
    key, value = shift_by_core(key, RING, -1), shift_by_core(value, RING, 1)
    weights = [weight] + [shift_by_core(weight, RING, by) for by in (-1, 2, 1)]
    part = kernel_call(near_body, shape((8, 32, 1024), BF16), [VMEM] * 3)(keep, key, value)
    far = lax.all_to_all(part, ("zh", "zm"), 0, 0, tiled=True)

    keep, ahead, across, behind = kernel_call(
        input_body,
        (shape((192, 1024), F32),) + (shape((192, 1024), BF16),) * 3,
        [SMEM] + [VMEM] * 6,
        scratch=[pltpu.VMEM((2, 4, 2, 32, 1024), BF16)],
        flops=10**11,
    )(place, own, twin, *weights)
    parts = [
        shift_by_core(ahead, line, 1),
        shift(across, "x", 2),
        shift_by_core(behind, line, -1),
    ]

    weight_sum, input_sum, peaks = kernel_call(
        peak_body,
        (shape((32, 1024), F32), shape((192, 1024), F32), shape((32, 128), F32)),
        [VMEM] * 5,
    )(far, keep, *parts)
    peaks = lax.all_to_all(peaks, ("x", *TENSOR), 0, 0, tiled=True)
    peaks = spread(jnp.max(peaks, axis=0), RING)
    grad_input, grad_key_weight, grad_value_weight, pair, one = kernel_call(
        final_body,
        (
            shape((192, 1024), BF16),
            shape((16, 1024), BF16),
            shape((16, 1024), BF16),
            shape((2,), F32),
            shape((1,), F32),
        ),
        [VMEM] * 3,
        (VMEM, VMEM, VMEM, SMEM, SMEM),
    )(peaks.reshape(16, 128), weight_sum, input_sum)
    return (grad_input, grad_key_weight.T, grad_value_weight.T, pair, one)


def solution(mesh):
    whole = Mesh(mesh.devices.reshape(4, 2, 2, 4, 4, 2), (*DP, *TENSOR))
    in_specs = (
        P(DP, TENSOR),
        P(DP, TENSOR),
        P(TENSOR, DP),
        P(TENSOR, DP),
        P(TENSOR, DP),
        P(TENSOR, DP),
        P(DP, TENSOR),
        P(DP, TENSOR),
    )
    out_specs = (P(DP, TENSOR), P(TENSOR, DP), P(TENSOR, DP), P(), P())
    return jax.shard_map(
        per_device, mesh=whole, in_specs=in_specs, out_specs=out_specs, check_vma=False
    )
```
